512 devices in a mesh: grp: 16 (over z, y_hi), seq: 32 (over x, y_lo, core).
Axes of the slice: x: 4, y: 8 (y_hi: 2, y_lo: 4; y = y_hi * 4 + y_lo), z: 8, core: 2. Of those that a mesh axis runs over, the one named last changes fastest.
Arguments:
- hidden: bfloat16 [512, 4096], P('seq'), may hold values from -1.5 to 1.5
- norm_gain: float32 [4096], replicated, may hold values from 0.25 to 1.75
- w_query: bfloat16 [4096, 2048], P('seq', 'grp'), may hold values from -0.09375 to 0.09375
- w_out: bfloat16 [2048, 4096], P('grp', 'seq'), may hold values from -0.125 to 0.125
- enc_cache: bfloat16 [2, 262144, 2048], P(None, 'seq', 'grp')
- lengths: int32 [512], replicated, may hold values from 1 to 262144, as said below
Outputs:
- mixed: bfloat16 [512, 4096], P('seq', 'grp')
The draws below stay inside these ranges and needn't reach their ends.
Inputs may be any that keep to these rules, and one draw needn't show every extreme that they name: `lengths`: every row has at least one valid position; some row in each draw has all 262144 positions valid.
All inputs are finite; a program needn't handle non-finite values.
Results may differ from the reference program's by a relative error of at most 0.02.
The reference program's roundings to bfloat16 on the way (of `normed`, `queries`, `weights` and `attended`) count: a program that leaves them out, or rounds other values in their place, can miss the bound.
Values may be sent and summed in bfloat16 or wider, within the bound.
A program may use at most 64 MiB of HBM per device.

```python
import jax
import jax.numpy as jnp
from jax import lax

D = 4096
HEAD_DIM = 64
HEADS = 32
ENC = 262144
TARGET = 512


def draw_enc_cache(key, part):
    key = jax.random.fold_in(key, 11)
    key_noise, value_noise = jax.random.split(key, 2)
    keys_part = 0.4 * jax.random.normal(key_noise, (ENC, HEADS * HEAD_DIM), jnp.float32)
    values_part = jax.random.normal(value_noise, (ENC, HEADS * HEAD_DIM), jnp.float32)
    return jnp.stack([keys_part, values_part]).astype(jnp.bfloat16)


def draw_lengths(key, part):
    key = jax.random.fold_in(key, 23)
    key_len, key_row = jax.random.split(key)
    drawn = jax.random.randint(key_len, (TARGET,), 1, ENC + 1, jnp.int32)
    chosen = jax.random.randint(key_row, (), 0, TARGET, jnp.int32)
    rows_index = jnp.arange(TARGET, dtype=jnp.int32)
    return jnp.where(rows_index == chosen, jnp.int32(ENC), drawn)


def shard_levels(rng, dims, pieces, smallest, high):
    factor_of, own = 1.0, jax.random.fold_in(rng, 6)
    for dim, shards_of in pieces:
        heights = jnp.exp(jax.random.uniform(jax.random.fold_in(own, dim), (shards_of,), jnp.float32, smallest / len(pieces), high / len(pieces)))
        factor_of = factor_of * jnp.repeat(heights, dims[dim] // shards_of).reshape([-1 if axis == dim else 1 for axis in range(len(dims))])
    return factor_of


def noise(key, shape, deviation, most, shards=(), held_as=jnp.bfloat16):
    values = deviation * jax.random.normal(key, shape, jnp.float32)
    if shards:
        values = values * shard_levels(key, shape, shards, -0.22, 0.18)
    return jnp.clip(values, -most, most).astype(held_as)


def setup_inputs(seed: int = 0) -> dict:
    seeds = jax.random.split(jax.random.key(seed), 7)
    hidden = noise(seeds[0], (TARGET, D), 0.25, 1.5, ((0, 32),))
    norm_gain = jnp.clip(1.0 + 0.15 * jax.random.normal(seeds[1], (D,), jnp.float32), 0.25, 1.75)
    w_query = noise(seeds[2], (D, HEADS * HEAD_DIM), D ** -0.5, 0.09375, ((0, 32), (1, 16)))
    w_out = noise(seeds[3], (HEADS * HEAD_DIM, D), (HEADS * HEAD_DIM) ** -0.5, 0.125, ((0, 16), (1, 32)))
    enc_cache = draw_enc_cache(jax.random.fold_in(seeds[6], 71), 0)
    lengths = draw_lengths(jax.random.fold_in(seeds[6], 71), 0)
    return dict(hidden=hidden, norm_gain=norm_gain, w_query=w_query, w_out=w_out, enc_cache=enc_cache, lengths=lengths)


def reference(hidden, norm_gain, w_query, w_out, enc_cache, lengths):
    wide = hidden.astype(jnp.float32)
    scale = lax.rsqrt(lax.optimization_barrier(jnp.mean(wide * wide, axis=-1, keepdims=True)) + 1e-06)
    normed = (wide * scale * norm_gain).astype(jnp.bfloat16)
    queries = jnp.dot(normed, w_query, preferred_element_type=jnp.float32).astype(jnp.bfloat16)
    positions = jnp.arange(ENC, dtype=jnp.int32)
    valid = positions[None, :] < lengths[:, None]

    def one_head(head):
        first = (head * HEAD_DIM).astype(jnp.int32)
        query_head = lax.dynamic_slice_in_dim(queries, first, HEAD_DIM, 1)
        key_head = lax.dynamic_slice_in_dim(enc_cache[0], first, HEAD_DIM, 1)
        value_head = lax.dynamic_slice_in_dim(enc_cache[1], first, HEAD_DIM, 1)
        score = jnp.dot(query_head, key_head.T, preferred_element_type=jnp.float32)
        masked = jnp.where(valid, score, jnp.float32(-1e+30))
        peak = lax.optimization_barrier(jnp.max(masked, axis=-1, keepdims=True))
        weights = jnp.where(valid, jnp.exp(score - peak), jnp.float32(0.0))
        total = lax.optimization_barrier(jnp.sum(weights, axis=-1, keepdims=True))
        summed = jnp.dot(weights.astype(jnp.bfloat16), value_head, preferred_element_type=jnp.float32)
        return summed / total
    heads_out = lax.map(one_head, jnp.arange(HEADS, dtype=jnp.int32))
    attended = heads_out.transpose(1, 0, 2).reshape(TARGET, HEADS * HEAD_DIM).astype(jnp.bfloat16)
    projected = jnp.dot(attended, w_out, preferred_element_type=jnp.float32)
    return (wide + projected).astype(jnp.bfloat16)
```

```python
import jax
import jax.numpy as jnp
from jax import lax
from jax.experimental import pallas as pl
from jax.experimental.pallas import tpu as pltpu
from jax.sharding import PartitionSpec as P

MESH = pl.DeviceIdType.MESH
F32 = jnp.float32
BF16 = jnp.bfloat16
NT = (((1,), (1,)), ((), ()))
LOG2E = 1.4426950408889634
NEG = -1e30
HEAD = 64
ROWS = 16
POS = 8192
CHUNK = 4096
WIDE = 64
VROWS = 144


def kernel(
    hid_h, gain_h, wq_h, wo_h, enc_h, len_h, out,
    hid, gain, wq, lens, kbuf, vbuf, vt, nrm, nra, wqa, prt, prs, qall, qw0, qw1, s0, s1,
    msg, cmb, rep, pick, att, wo,
    load, wq_s, wq_r, nr_s, nr_r, ps_s, ps_r, q_s, q_r, m_s, m_r, a_s, a_r, t_s, t_r, y_s, y_r, x_s, x_r, c_s, c_r,
):
    s, g = lax.axis_index("seq"), lax.axis_index("grp")
    x, yc, p, c = s // 8, s % 8, s // 2, s % 2
    y = yc // 2
    apart = p != g
    turned = {"seq": 2 * g + c, "grp": p}

    def send(src, dst, ssem, rsem, where):
        return pltpu.make_async_remote_copy(
            src_ref=src, dst_ref=dst, send_sem=ssem, recv_sem=rsem, device_id=where, device_id_type=MESH
        )

    loads = [
        pltpu.make_async_copy(a, b, load.at[i])
        for i, (a, b) in enumerate(
            [(hid_h, hid), (gain_h, gain), (wq_h, wq), (len_h, lens), (enc_h.at[1], vbuf), (enc_h.at[0], kbuf)]
        )
    ]
    for one in loads:
        one.start()
    barrier = pltpu.get_barrier_semaphore()
    for o in range(1, 32):
        pl.semaphore_signal(barrier, inc=1, device_id={"seq": (s + o) % 32}, device_id_type=MESH)
    for o in range(1, 16):
        pl.semaphore_signal(barrier, inc=1, device_id={"grp": (g + o) % 16}, device_id_type=MESH)

    @pl.when(apart)
    def _():
        pl.semaphore_signal(barrier, inc=1, device_id=turned, device_id_type=MESH)

    loads[0].wait()
    loads[1].wait()
    loads[2].wait()
    wide = hid[...].astype(F32)
    scale = lax.rsqrt(jnp.mean(wide * wide, axis=-1, keepdims=True) + 1e-06)
    normed = (wide * scale * gain[...]).astype(BF16)
    for i in range(8):
        nrm[i] = jnp.concatenate([normed[:, j * 1024 + i * 128 : j * 1024 + i * 128 + 128] for j in range(4)], axis=1)
    nra[yc] = nrm[yc]
    wqa[x] = wq[...]

    pl.semaphore_wait(barrier, 46 + apart.astype(jnp.int32))

    gathers, sends = [], []
    for o in range(1, 8):
        to, other = (yc + o) % 8, (yc + 8 - o) % 8
        sends.append(send(nrm.at[to], nra.at[yc], nr_s.at[o], nr_r.at[yc], {"seq": x * 8 + to}))
        gathers.append(send(nrm.at[to], nra.at[other], nr_s.at[o], nr_r.at[other], {"seq": x * 8 + to}))
    for o in range(1, 4):
        to, other = (x + o) % 4, (x + 4 - o) % 4
        sends.append(send(wq, wqa.at[x], wq_s.at[o], wq_r.at[x], {"seq": to * 8 + yc}))
        gathers.append(send(wq, wqa.at[other], wq_s.at[o], wq_r.at[other], {"seq": to * 8 + yc}))
    for one in sends:
        one.start()

    turn = send(wo_h, wo.at[c, g], t_s, t_r, turned)
    stay = pltpu.make_async_copy(wo_h, wo.at[c, g], t_s)

    @pl.when(apart)
    def _():
        turn.start()

    @pl.when(jnp.logical_not(apart))
    def _():
        stay.start()

    loads[4].wait()
    for i in range(8):
        vt[0:128, i * 1024 : (i + 1) * 1024] = vbuf[i * 1024 : (i + 1) * 1024, :].T
    vt[128:VROWS, :] = jnp.ones((VROWS - 128, POS), BF16)
    row = lax.broadcasted_iota(jnp.int32, (64, 4096), 0)
    col = lax.broadcasted_iota(jnp.int32, (64, 4096), 1)
    rep[...] = ((row % 32 == col // 128) & (row // 32 == (col % 128) // HEAD)).astype(F32).astype(BF16)
    row = lax.broadcasted_iota(jnp.int32, (64, 512), 0)
    col = lax.broadcasted_iota(jnp.int32, (64, 512), 1)
    pick[...] = ((row % 32 == col // 16) & (col % 16 < 6) & (col % 2 == row // 32)).astype(F32).astype(BF16)
    loads[3].wait()

    for one in gathers:
        one.wait_recv()
    part = jnp.dot(nra[...].reshape(128, 512), wqa[...].reshape(512, 128), preferred_element_type=F32)
    prt[...] = part.reshape(8, ROWS, 128)
    prs[yc] = prt[yc]
    gathers = []
    for o in range(1, 8):
        to, other = (yc + o) % 8, (yc + 8 - o) % 8
        one = send(prt.at[to], prs.at[yc], ps_s.at[o], ps_r.at[yc], {"seq": x * 8 + to})
        one.start()
        sends.append(one)
        gathers.append(send(prt.at[to], prs.at[other], ps_s.at[o], ps_r.at[other], {"seq": x * 8 + to}))
    for one in gathers:
        one.wait_recv()
    total = prs[0]
    for i in range(1, 8):
        total = total + prs[i]
    qall[s] = total.astype(BF16)

    def plane(k):
        return (x + k) % 4

    for k in (0, 3, 2, 1):
        for o in range(1 if k == 0 else 0, 8):
            to = plane(k) * 8 + (yc + o) % 8
            one = send(qall.at[s], qall.at[s], q_s.at[k * 8 + o], q_r.at[s], {"seq": to})
            one.start()
            sends.append(one)

    lane = lax.broadcasted_iota(jnp.int32, (128, 128), 1)
    qws, sbufs = (qw0, qw1), (s0, s1)

    def take_queries(k):
        for o in range(1 if k == 0 else 0, 8):
            at = plane(k) * 8 + (yc + o) % 8
            send(qall.at[s], qall.at[at], q_s.at[0], q_r.at[at], {"seq": (s + 1) % 32}).wait_recv()
        q = qall[pl.ds(plane(k) * 8, 8)].reshape(128, 128).astype(F32) * LOG2E
        high = q.astype(BF16).astype(F32)
        low = q - high
        qw = qws[k % 2]
        for h in range(2):
            keep = (lane < HEAD) if h == 0 else (lane >= HEAD)
            qw[h * 128 : (h + 1) * 128, 0:128] = jnp.where(keep, high, 0.0).astype(BF16)
            qw[h * 128 : (h + 1) * 128, 128:256] = jnp.where(keep, low, 0.0).astype(BF16)

    def scores(k, i, top):
        keys = kbuf[pl.ds(i * CHUNK, CHUNK), :]
        keys = jnp.concatenate([keys, keys], axis=1)
        score = lax.dot_general(keys, qws[k % 2][...], NT, preferred_element_type=F32)
        left = lens[pl.ds(plane(k), 1), :] - s * POS - i * CHUNK
        ok = lax.broadcasted_iota(jnp.int32, (CHUNK, 128), 0) < left
        score = jnp.concatenate(
            [jnp.where(ok, score[:, :128], NEG), jnp.where(ok, score[:, 128:], NEG)], axis=1
        )
        sbufs[k % 2][pl.ds(i * CHUNK, CHUNK), :] = score
        return jnp.maximum(top, score.reshape(CHUNK // WIDE, WIDE, 256).max(axis=0))

    def weigh(k, i, peak, acc):
        weights = jnp.exp2(sbufs[k % 2][pl.ds(i * CHUNK, CHUNK), :] - peak).astype(BF16)
        values = vt[:, pl.ds(pl.multiple_of(i * CHUNK, CHUNK), CHUNK)]
        return acc + jnp.dot(values, weights, preferred_element_type=F32)

    def deliver(k, peak, acc):
        total = acc[128:129, :]
        scale = 1.0 / total
        both = jnp.concatenate(
            [acc[0:64, 0:128] * scale[:, 0:128], acc[64:128, 128:256] * scale[:, 128:256]], axis=0
        )
        msg[k, :, 0:ROWS, :] = both.T.astype(BF16).reshape(8, ROWS, 128)
        level = peak + jnp.log2(total)
        high = level.astype(BF16).astype(F32)
        mid = (level - high).astype(BF16).astype(F32)
        low = level - high - mid
        rows = [v[:, h * 128 : (h + 1) * 128] for v in (high, mid, low) for h in range(2)]
        rows = jnp.concatenate(rows + [jnp.zeros((10, 128), F32)], axis=0).astype(BF16)
        for o in range(8):
            msg[k, o, ROWS : 2 * ROWS, :] = rows
        if k == 0:
            cmb[s] = msg[0, yc]
        for o in range(1 if k == 0 else 0, 8):
            to = (yc + o) % 8
            one = send(msg.at[k, to], cmb.at[s], m_s.at[k * 8 + o], m_r.at[s], {"seq": plane(k) * 8 + to})
            one.start()
            sends.append(one)

    def background(stage):
        if stage == 0:
            pl.when(apart)(turn.wait_recv)
            pl.when(jnp.logical_not(apart))(stay.wait)
            for o in range(1, 4):
                to = x * 8 + ((y + o) % 4) * 2 + c
                one = send(wo.at[c, p], wo.at[c, p], y_s.at[o], y_r.at[y], {"seq": to})
                one.start()
                sends.append(one)
        if stage == 1:
            for o in range(1, 4):
                at = (y + o) % 4
                slot = wo.at[c, x * 4 + at]
                send(slot, slot, y_s.at[0], y_r.at[at], {"seq": (s + 1) % 32}).wait_recv()
            for o in range(1, 4):
                to = ((x + o) % 4) * 8 + yc
                four = wo.at[c, pl.ds(x * 4, 4)]
                one = send(four, four, x_s.at[o], x_r.at[x], {"seq": to})
                one.start()
                sends.append(one)
        if stage == 3:
            for o in range(1, 4):
                at = (x + o) % 4
                four = wo.at[c, pl.ds(at * 4, 4)]
                send(four, four, x_s.at[0], x_r.at[at], {"seq": (s + 1) % 32}).wait_recv()
            one = send(wo.at[c], wo.at[c], c_s, c_r, {"seq": s + 1 - 2 * c})
            one.start()
            sends.append(one)

    loads[5].wait()
    peak = None
    for stage in range(5):
        if stage < 4:
            take_queries(stage)

        def step(i, carry, stage=stage, peak=peak):
            top, acc = carry
            if stage < 4:
                top = scores(stage, i, top)
            if stage > 0:
                acc = weigh(stage - 1, i, peak, acc)
            return top, acc

        top, acc = lax.fori_loop(
            0, POS // CHUNK, step, (jnp.full((WIDE, 256), NEG, F32), jnp.zeros((VROWS, 256), F32))
        )
        if stage > 0:
            deliver(stage - 1, peak, acc)
        if stage < 4:
            peak = jnp.max(top, axis=0, keepdims=True)
        background(stage)

    for o in range(1, 32):
        at = (s + o) % 32
        send(cmb.at[at], cmb.at[at], m_s.at[0], m_r.at[at], {"seq": (s + 1) % 32}).wait_recv()
    level = jnp.dot(pick[...], cmb[:, ROWS : 2 * ROWS, :].reshape(512, 128), preferred_element_type=F32)
    shares = []
    for h in range(2):
        one = level[h * 32 : (h + 1) * 32]
        one = jnp.exp2(one - jnp.max(one, axis=0, keepdims=True))
        shares.append(one / jnp.sum(one, axis=0, keepdims=True))
    share = jnp.concatenate(shares, axis=0)
    high = share.astype(BF16)
    low = (share - high.astype(F32)).astype(BF16)
    own = (
        lax.broadcasted_iota(jnp.int32, (ROWS, 128), 1) == yc * ROWS + lax.broadcasted_iota(jnp.int32, (ROWS, 128), 0)
    ).astype(F32).astype(BF16)
    turned_share = lax.dot_general(own, high, NT, preferred_element_type=F32) + lax.dot_general(
        own, low, NT, preferred_element_type=F32
    )
    high = turned_share.astype(BF16)
    low = (turned_share - high.astype(F32)).astype(BF16)
    spread = jnp.dot(high, rep[...], preferred_element_type=F32) + jnp.dot(low, rep[...], preferred_element_type=F32)
    joined = jnp.zeros((ROWS, 128), F32)
    for i in range(32):
        joined = joined + spread[:, i * 128 : (i + 1) * 128] * cmb[i, 0:ROWS, :].astype(F32)
    att[g] = joined.astype(BF16)
    for o in range(1, 16):
        one = send(att.at[g], att.at[g], a_s.at[o], a_r.at[g], {"grp": (g + o) % 16})
        one.start()
        sends.append(one)
    send(wo.at[1 - c], wo.at[1 - c], c_s, c_r, {"seq": s + 1 - 2 * c}).wait_recv()
    for o in range(1, 16):
        at = (g + o) % 16
        send(att.at[at], att.at[at], a_s.at[0], a_r.at[at], {"grp": (g + 1) % 16}).wait_recv()
    attended = jnp.concatenate([att[i] for i in range(16)], axis=1)
    for h in range(2):
        mixed = jnp.dot(attended, wo[h].reshape(2048, 128), preferred_element_type=F32)
        base = hid[:, pl.ds(pl.multiple_of(g * 256 + h * 128, 128), 128)].astype(F32)
        out[:, h * 128 : (h + 1) * 128] = (base + mixed).astype(BF16)

    for one in sends:
        one.wait_send()
    pl.when(apart)(turn.wait_send)


def body(hidden, norm_gain, w_query, w_out, enc_cache, lengths):
    dma = pltpu.SemaphoreType.DMA
    vm = pltpu.VMEM
    any_space = pl.BlockSpec(memory_space=pl.ANY)
    return pl.pallas_call(
        kernel,
        out_shape=jax.ShapeDtypeStruct((ROWS, 256), BF16),
        in_specs=[any_space] * 6,
        out_specs=pl.BlockSpec(memory_space=pltpu.VMEM),
        scratch_shapes=[
            vm((ROWS, 4096), BF16), vm((1, 4096), F32), vm((128, 128), BF16), vm((4, 128), jnp.int32),
            vm((POS, 128), BF16), vm((POS, 128), BF16), vm((VROWS, POS), BF16),
            vm((8, ROWS, 512), BF16), vm((8, ROWS, 512), BF16), vm((4, 128, 128), BF16),
            vm((8, ROWS, 128), F32), vm((8, ROWS, 128), F32), vm((32, ROWS, 128), BF16),
            vm((256, 256), BF16), vm((256, 256), BF16), vm((POS, 256), F32), vm((POS, 256), F32),
            vm((4, 8, 2 * ROWS, 128), BF16), vm((32, 2 * ROWS, 128), BF16), vm((64, 4096), BF16), vm((64, 512), BF16),
            vm((16, ROWS, 128), BF16), vm((2, 16, 128, 128), BF16),
            dma((6,)), dma((4,)), dma((4,)), dma((8,)), dma((8,)), dma((8,)), dma((8,)), dma((32,)), dma((32,)),
            dma((32,)), dma((32,)), dma((16,)), dma((16,)), dma, dma, dma((4,)), dma((4,)), dma((4,)), dma((4,)), dma, dma,
        ],
        compiler_params=pltpu.CompilerParams(
            collective_id=0, has_side_effects=True, vmem_limit_bytes=56 * 2**20
        ),
        cost_estimate=pl.CostEstimate(flops=2200000000, bytes_accessed=6000000, transcendentals=8400000),
    )(hidden, norm_gain.reshape(1, 4096), w_query, w_out, enc_cache, lengths.reshape(4, 128))


def solution(mesh):
    placed = (P("seq", None), P(), P("seq", "grp"), P("grp", "seq"), P(None, "seq", "grp"), P())
    return jax.shard_map(body, mesh=mesh, in_specs=placed, out_specs=P("seq", "grp"), check_vma=False)
```

```python
import jax
import jax.numpy as jnp
from jax import lax
from jax.experimental import pallas as pl
from jax.experimental.pallas import tpu as pltpu
from jax.sharding import PartitionSpec as P

MESH = pl.DeviceIdType.MESH
F32 = jnp.float32
BF16 = jnp.bfloat16
NT = (((1,), (1,)), ((), ()))
LOG2E = 1.4426950408889634
NEG = -1e30
HEAD = 64
ROWS = 16
POS = 8192
CHUNK = 4096
WIDE = 64
VROWS = 144


def kernel(
    hid_h, gain_h, wq_h, wo_h, enc_h, len_h, out,
    hid, gain, wq, lens_in, lens, kbuf, vbuf, vt, nrm, nra, wqa, prt, prs, qall, qw0, qw1, s0, s1,
    msg, cmb, rep, pick, att, wo,
    load, wq_s, wq_r, nr_s, nr_r, ps_s, ps_r, q_s, q_r, m_s, m_r, a_s, a_r, t_s, t_r, w_s, w_r, c_s, c_r,
):
    s, g = lax.axis_index("seq"), lax.axis_index("grp")
    x, y, p, c = s // 8, (s // 2) % 4, s // 2, s % 2
    e = x * 2 + c
    apart = p != g
    turned = {"seq": 2 * g + c, "grp": p}

    def at_y(place, row):
        return (place // 2) * 8 + row * 2 + place % 2

    def send(src, dst, ssem, rsem, where):
        return pltpu.make_async_remote_copy(
            src_ref=src, dst_ref=dst, send_sem=ssem, recv_sem=rsem, device_id=where, device_id_type=MESH
        )

    loads = [
        pltpu.make_async_copy(a, b, load.at[i])
        for i, (a, b) in enumerate(
            [(hid_h, hid), (gain_h, gain), (wq_h, wq), (len_h, lens_in), (enc_h.at[1], vbuf), (enc_h.at[0], kbuf)]
        )
    ]
    for one in loads:
        one.start()
    barrier = pltpu.get_barrier_semaphore()
    for o in range(1, 32):
        pl.semaphore_signal(barrier, inc=1, device_id={"seq": (s + o) % 32}, device_id_type=MESH)
    for o in range(1, 16):
        pl.semaphore_signal(barrier, inc=1, device_id={"grp": (g + o) % 16}, device_id_type=MESH)

    @pl.when(apart)
    def _():
        pl.semaphore_signal(barrier, inc=1, device_id=turned, device_id_type=MESH)

    loads[0].wait()
    loads[1].wait()
    loads[2].wait()
    wide = hid[...].astype(F32)
    scale = lax.rsqrt(jnp.mean(wide * wide, axis=-1, keepdims=True) + 1e-06)
    normed = (wide * scale * gain[...]).astype(BF16)
    for i in range(8):
        nrm[i] = jnp.concatenate([normed[:, at_y(i, j) * 128 : at_y(i, j) * 128 + 128] for j in range(4)], axis=1)
    nra[e] = nrm[e]
    wqa[y] = wq[...]

    pl.semaphore_wait(barrier, 46 + apart.astype(jnp.int32))

    gathers, sends = [], []
    for o in range(1, 4):
        to, other = (y + o) % 4, (y + 4 - o) % 4
        sends.append(send(wq, wqa.at[y], wq_s.at[o], wq_r.at[y], {"seq": at_y(e, to)}))
        gathers.append(send(wq, wqa.at[other], wq_s.at[o], wq_r.at[other], {"seq": at_y(e, to)}))
    for o in range(1, 8):
        to, other = (e + o) % 8, (e + 8 - o) % 8
        sends.append(send(nrm.at[to], nra.at[e], nr_s.at[o], nr_r.at[e], {"seq": at_y(to, y)}))
        gathers.append(send(nrm.at[to], nra.at[other], nr_s.at[o], nr_r.at[other], {"seq": at_y(to, y)}))
    for one in sends:
        one.start()

    turn = send(wo_h, wo.at[c, g], t_s, t_r, turned)
    stay = pltpu.make_async_copy(wo_h, wo.at[c, g], t_s)

    @pl.when(apart)
    def _():
        turn.start()

    @pl.when(jnp.logical_not(apart))
    def _():
        stay.start()

    loads[4].wait()
    for i in range(8):
        vt[0:128, i * 1024 : (i + 1) * 1024] = vbuf[i * 1024 : (i + 1) * 1024, :].T
    vt[128:VROWS, :] = jnp.ones((VROWS - 128, POS), BF16)
    row = lax.broadcasted_iota(jnp.int32, (64, 4096), 0)
    col = lax.broadcasted_iota(jnp.int32, (64, 4096), 1)
    rep[...] = ((row % 32 == col // 128) & (row // 32 == (col % 128) // HEAD)).astype(F32).astype(BF16)
    row = lax.broadcasted_iota(jnp.int32, (64, 512), 0)
    col = lax.broadcasted_iota(jnp.int32, (64, 512), 1)
    pick[...] = ((row % 32 == col // 16) & (col % 16 < 6) & (col % 2 == row // 32)).astype(F32).astype(BF16)
    loads[3].wait()
    for i in range(4):
        lens[i : i + 1, :] = jnp.concatenate([lens_in[j : j + 1, i * 32 : i * 32 + 32] for j in range(4)], axis=1)

    for one in gathers:
        one.wait_recv()
    part = jnp.dot(nra[...].reshape(128, 512), wqa[...].reshape(512, 128), preferred_element_type=F32)
    prt[...] = part.reshape(8, ROWS, 128)
    prs[e] = prt[e]
    gathers = []
    for o in range(1, 8):
        to, other = (e + o) % 8, (e + 8 - o) % 8
        one = send(prt.at[to], prs.at[e], ps_s.at[o], ps_r.at[e], {"seq": at_y(to, y)})
        one.start()
        sends.append(one)
        gathers.append(send(prt.at[to], prs.at[other], ps_s.at[o], ps_r.at[other], {"seq": at_y(to, y)}))
    for one in gathers:
        one.wait_recv()
    total = prs[0]
    for i in range(1, 8):
        total = total + prs[i]
    me = y * 8 + e
    qall[me] = total.astype(BF16)
    order = (0, 2, 3, 1)

    def group(k):
        return y ^ order[k]

    for k in range(4):
        for o in range(1 if k == 0 else 0, 8):
            one = send(
                qall.at[me], qall.at[me], q_s.at[k * 8 + o], q_r.at[me], {"seq": at_y((e + o) % 8, group(k))}
            )
            one.start()
            sends.append(one)

    pl.when(apart)(turn.wait_recv)
    pl.when(jnp.logical_not(apart))(stay.wait)
    for o in range(1, 16):
        one = send(wo.at[c, p], wo.at[c, p], w_s.at[o], w_r.at[p], {"seq": 2 * ((p + o) % 16) + c})
        one.start()
        sends.append(one)

    lane = lax.broadcasted_iota(jnp.int32, (128, 128), 1)
    qws, sbufs = (qw0, qw1), (s0, s1)

    def take_queries(k):
        for o in range(1 if k == 0 else 0, 8):
            at = group(k) * 8 + (e + o) % 8
            send(qall.at[s], qall.at[at], q_s.at[0], q_r.at[at], {"seq": (s + 1) % 32}).wait_recv()
        q = qall[pl.ds(group(k) * 8, 8)].reshape(128, 128).astype(F32) * LOG2E
        high = q.astype(BF16).astype(F32)
        low = q - high
        qw = qws[k % 2]
        for h in range(2):
            keep = (lane < HEAD) if h == 0 else (lane >= HEAD)
            qw[h * 128 : (h + 1) * 128, 0:128] = jnp.where(keep, high, 0.0).astype(BF16)
            qw[h * 128 : (h + 1) * 128, 128:256] = jnp.where(keep, low, 0.0).astype(BF16)

    def scores(k, i, top):
        keys = kbuf[pl.ds(i * CHUNK, CHUNK), :]
        keys = jnp.concatenate([keys, keys], axis=1)
        score = lax.dot_general(keys, qws[k % 2][...], NT, preferred_element_type=F32)
        left = lens[pl.ds(group(k), 1), :] - s * POS - i * CHUNK
        ok = lax.broadcasted_iota(jnp.int32, (CHUNK, 128), 0) < left
        score = jnp.concatenate(
            [jnp.where(ok, score[:, :128], NEG), jnp.where(ok, score[:, 128:], NEG)], axis=1
        )
        sbufs[k % 2][pl.ds(i * CHUNK, CHUNK), :] = score
        return jnp.maximum(top, score.reshape(CHUNK // WIDE, WIDE, 256).max(axis=0))

    def weigh(k, i, peak, acc):
        weights = jnp.exp2(sbufs[k % 2][pl.ds(i * CHUNK, CHUNK), :] - peak).astype(BF16)
        values = vt[:, pl.ds(pl.multiple_of(i * CHUNK, CHUNK), CHUNK)]
        return acc + jnp.dot(values, weights, preferred_element_type=F32)

    def deliver(k, peak, acc):
        total = acc[128:129, :]
        scale = 1.0 / total
        both = jnp.concatenate(
            [acc[0:64, 0:128] * scale[:, 0:128], acc[64:128, 128:256] * scale[:, 128:256]], axis=0
        )
        msg[k, :, 0:ROWS, :] = both.T.astype(BF16).reshape(8, ROWS, 128)
        level = peak + jnp.log2(total)
        high = level.astype(BF16).astype(F32)
        mid = (level - high).astype(BF16).astype(F32)
        low = level - high - mid
        rows = [v[:, h * 128 : (h + 1) * 128] for v in (high, mid, low) for h in range(2)]
        rows = jnp.concatenate(rows + [jnp.zeros((10, 128), F32)], axis=0).astype(BF16)
        for o in range(8):
            msg[k, o, ROWS : 2 * ROWS, :] = rows
        if k == 0:
            cmb[s] = msg[0, e]
        for o in range(1 if k == 0 else 0, 8):
            to = (e + o) % 8
            one = send(msg.at[k, to], cmb.at[s], m_s.at[k * 8 + o], m_r.at[s], {"seq": at_y(to, group(k))})
            one.start()
            sends.append(one)

    loads[5].wait()
    peak = None
    for stage in range(5):
        if stage < 4:
            take_queries(stage)

        def step(i, carry, stage=stage, peak=peak):
            top, acc = carry
            if stage < 4:
                top = scores(stage, i, top)
            if stage > 0:
                acc = weigh(stage - 1, i, peak, acc)
            return top, acc

        top, acc = lax.fori_loop(
            0, POS // CHUNK, step, (jnp.full((WIDE, 256), NEG, F32), jnp.zeros((VROWS, 256), F32))
        )
        if stage > 0:
            deliver(stage - 1, peak, acc)
        if stage < 4:
            peak = jnp.max(top, axis=0, keepdims=True)

    for o in range(1, 16):
        at = (p + o) % 16
        send(wo.at[c, at], wo.at[c, at], w_s.at[0], w_r.at[at], {"seq": (s + 1) % 32}).wait_recv()
    swap = send(wo.at[c], wo.at[c], c_s, c_r, {"seq": s + 1 - 2 * c})
    swap.start()
    sends.append(swap)

    for o in range(1, 32):
        at = (s + o) % 32
        send(cmb.at[at], cmb.at[at], m_s.at[0], m_r.at[at], {"seq": (s + 1) % 32}).wait_recv()
    level = jnp.dot(pick[...], cmb[:, ROWS : 2 * ROWS, :].reshape(512, 128), preferred_element_type=F32)
    shares = []
    for h in range(2):
        one = level[h * 32 : (h + 1) * 32]
        one = jnp.exp2(one - jnp.max(one, axis=0, keepdims=True))
        shares.append(one / jnp.sum(one, axis=0, keepdims=True))
    share = jnp.concatenate(shares, axis=0)
    high = share.astype(BF16)
    low = (share - high.astype(F32)).astype(BF16)
    own = (
        lax.broadcasted_iota(jnp.int32, (ROWS, 128), 1) == e * ROWS + lax.broadcasted_iota(jnp.int32, (ROWS, 128), 0)
    ).astype(F32).astype(BF16)
    turned_share = lax.dot_general(own, high, NT, preferred_element_type=F32) + lax.dot_general(
        own, low, NT, preferred_element_type=F32
    )
    high = turned_share.astype(BF16)
    low = (turned_share - high.astype(F32)).astype(BF16)
    spread = jnp.dot(high, rep[...], preferred_element_type=F32) + jnp.dot(low, rep[...], preferred_element_type=F32)
    joined = jnp.zeros((ROWS, 128), F32)
    for i in range(32):
        joined = joined + spread[:, i * 128 : (i + 1) * 128] * cmb[i, 0:ROWS, :].astype(F32)
    att[g] = joined.astype(BF16)
    for o in range(1, 16):
        one = send(att.at[g], att.at[g], a_s.at[o], a_r.at[g], {"grp": (g + o) % 16})
        one.start()
        sends.append(one)
    send(wo.at[1 - c], wo.at[1 - c], c_s, c_r, {"seq": s + 1 - 2 * c}).wait_recv()
    for o in range(1, 16):
        at = (g + o) % 16
        send(att.at[at], att.at[at], a_s.at[0], a_r.at[at], {"grp": (g + 1) % 16}).wait_recv()
    attended = jnp.concatenate([att[i] for i in range(16)], axis=1)
    for h in range(2):
        mixed = jnp.dot(attended, wo[h].reshape(2048, 128), preferred_element_type=F32)
        base = hid[:, pl.ds(pl.multiple_of(g * 256 + h * 128, 128), 128)].astype(F32)
        out[:, h * 128 : (h + 1) * 128] = (base + mixed).astype(BF16)

    for one in sends:
        one.wait_send()
    pl.when(apart)(turn.wait_send)


def body(hidden, norm_gain, w_query, w_out, enc_cache, lengths):
    dma = pltpu.SemaphoreType.DMA
    vm = pltpu.VMEM
    any_space = pl.BlockSpec(memory_space=pl.ANY)
    return pl.pallas_call(
        kernel,
        out_shape=jax.ShapeDtypeStruct((ROWS, 256), BF16),
        in_specs=[any_space] * 6,
        out_specs=pl.BlockSpec(memory_space=pltpu.VMEM),
        scratch_shapes=[
            vm((ROWS, 4096), BF16), vm((1, 4096), F32), vm((128, 128), BF16), vm((4, 128), jnp.int32), vm((4, 128), jnp.int32),
            vm((POS, 128), BF16), vm((POS, 128), BF16), vm((VROWS, POS), BF16),
            vm((8, ROWS, 512), BF16), vm((8, ROWS, 512), BF16), vm((4, 128, 128), BF16),
            vm((8, ROWS, 128), F32), vm((8, ROWS, 128), F32), vm((32, ROWS, 128), BF16),
            vm((256, 256), BF16), vm((256, 256), BF16), vm((POS, 256), F32), vm((POS, 256), F32),
            vm((4, 8, 2 * ROWS, 128), BF16), vm((32, 2 * ROWS, 128), BF16), vm((64, 4096), BF16), vm((64, 512), BF16),
            vm((16, ROWS, 128), BF16), vm((2, 16, 128, 128), BF16),
            dma((6,)), dma((4,)), dma((4,)), dma((8,)), dma((8,)), dma((8,)), dma((8,)), dma((32,)), dma((32,)),
            dma((32,)), dma((32,)), dma((16,)), dma((16,)), dma, dma, dma((16,)), dma((16,)), dma, dma,
        ],
        compiler_params=pltpu.CompilerParams(
            collective_id=0, has_side_effects=True, vmem_limit_bytes=56 * 2**20
        ),
        cost_estimate=pl.CostEstimate(flops=2200000000, bytes_accessed=6000000, transcendentals=8400000),
    )(hidden, norm_gain.reshape(1, 4096), w_query, w_out, enc_cache, lengths.reshape(4, 128))


def solution(mesh):
    placed = (P("seq", None), P(), P("seq", "grp"), P("grp", "seq"), P(None, "seq", "grp"), P())
    return jax.shard_map(body, mesh=mesh, in_specs=placed, out_specs=P("seq", "grp"), check_vma=False)
```

```python
import jax
import jax.numpy as jnp
from jax import lax
from jax.experimental import pallas as pl
from jax.experimental.pallas import tpu as pltpu
from jax.sharding import PartitionSpec as P

MESH = pl.DeviceIdType.MESH
F32 = jnp.float32
BF16 = jnp.bfloat16
NT = (((1,), (1,)), ((), ()))
LOG2E = 1.4426950408889634
NEG = -1e30
HEAD = 64
ROWS = 16
POS = 8192
CHUNK = 4096
WIDE = 64
VROWS = 144


def kernel(
    hid_h, gain_h, wq_h, wo_h, enc_h, len_h, out,
    hid, gain, wq, lens_in, lens, kbuf, vbuf, vt, nrm, nra, wqa, prt, prs, qall, qw0, qw1, s0, s1,
    msg, cmb, rep, pick, att, wo,
    load, wq_s, wq_r, nr_s, nr_r, ps_s, ps_r, q_s, q_r, m_s, m_r, a_s, a_r, t_s, t_r, w_s, w_r, c_s, c_r,
):
    s, g = lax.axis_index("seq"), lax.axis_index("grp")
    x, y, p, c = s // 8, (s // 2) % 4, s // 2, s % 2
    e = x * 2 + c
    apart = p != g
    turned = {"seq": 2 * g + c, "grp": p}

    def at_y(place, row):
        return (place // 2) * 8 + row * 2 + place % 2

    def send(src, dst, ssem, rsem, where):
        return pltpu.make_async_remote_copy(
            src_ref=src, dst_ref=dst, send_sem=ssem, recv_sem=rsem, device_id=where, device_id_type=MESH
        )

    loads = [
        pltpu.make_async_copy(a, b, load.at[i])
        for i, (a, b) in enumerate(
            [(hid_h, hid), (gain_h, gain), (wq_h, wq), (len_h, lens_in), (enc_h.at[1], vbuf), (enc_h.at[0], kbuf)]
        )
    ]
    for one in loads:
        one.start()
    barrier = pltpu.get_barrier_semaphore()
    for o in range(1, 8):
        pl.semaphore_signal(barrier, inc=1, device_id={"seq": at_y((e + o) % 8, y)}, device_id_type=MESH)
    for o in range(1, 4):
        pl.semaphore_signal(barrier, inc=1, device_id={"seq": at_y(e, (y + o) % 4)}, device_id_type=MESH)
    for o in range(1, 16):
        pl.semaphore_signal(barrier, inc=1, device_id={"grp": (g + o) % 16}, device_id_type=MESH)

    @pl.when(apart)
    def _():
        pl.semaphore_signal(barrier, inc=1, device_id=turned, device_id_type=MESH)

    loads[0].wait()
    loads[1].wait()
    loads[2].wait()
    wide = hid[...].astype(F32)
    scale = lax.rsqrt(jnp.mean(wide * wide, axis=-1, keepdims=True) + 1e-06)
    normed = (wide * scale * gain[...]).astype(BF16)
    for i in range(8):
        nrm[i] = jnp.concatenate([normed[:, at_y(i, j) * 128 : at_y(i, j) * 128 + 128] for j in range(4)], axis=1)
    nra[e] = nrm[e]
    wqa[y] = wq[...]

    pl.semaphore_wait(barrier, 25 + apart.astype(jnp.int32))

    gathers, sends = [], []
    for o in range(1, 4):
        to, other = (y + o) % 4, (y + 4 - o) % 4
        sends.append(send(wq, wqa.at[y], wq_s.at[o], wq_r.at[y], {"seq": at_y(e, to)}))
        gathers.append(send(wq, wqa.at[other], wq_s.at[o], wq_r.at[other], {"seq": at_y(e, to)}))
    for o in range(1, 8):
        to, other = (e + o) % 8, (e + 8 - o) % 8
        sends.append(send(nrm.at[to], nra.at[e], nr_s.at[o], nr_r.at[e], {"seq": at_y(to, y)}))
        gathers.append(send(nrm.at[to], nra.at[other], nr_s.at[o], nr_r.at[other], {"seq": at_y(to, y)}))
    for one in sends:
        one.start()

    loads[4].wait()
    for i in range(8):
        vt[0:128, i * 1024 : (i + 1) * 1024] = vbuf[i * 1024 : (i + 1) * 1024, :].T
    vt[128:VROWS, :] = jnp.ones((VROWS - 128, POS), BF16)
    row = lax.broadcasted_iota(jnp.int32, (64, 4096), 0)
    col = lax.broadcasted_iota(jnp.int32, (64, 4096), 1)
    rep[...] = ((row % 32 == col // 128) & (row // 32 == (col % 128) // HEAD)).astype(F32).astype(BF16)
    row = lax.broadcasted_iota(jnp.int32, (64, 512), 0)
    col = lax.broadcasted_iota(jnp.int32, (64, 512), 1)
    pick[...] = ((row % 32 == col // 16) & (col % 16 < 6) & (col % 2 == row // 32)).astype(F32).astype(BF16)
    loads[3].wait()
    for i in range(4):
        lens[i : i + 1, :] = jnp.concatenate([lens_in[j : j + 1, i * 32 : i * 32 + 32] for j in range(4)], axis=1)

    for one in gathers:
        one.wait_recv()
    part = jnp.dot(nra[...].reshape(128, 512), wqa[...].reshape(512, 128), preferred_element_type=F32)
    prt[...] = part.reshape(8, ROWS, 128)
    prs[e] = prt[e]
    gathers = []
    for o in range(1, 8):
        to, other = (e + o) % 8, (e + 8 - o) % 8
        one = send(prt.at[to], prs.at[e], ps_s.at[o], ps_r.at[e], {"seq": at_y(to, y)})
        one.start()
        sends.append(one)
        gathers.append(send(prt.at[to], prs.at[other], ps_s.at[o], ps_r.at[other], {"seq": at_y(to, y)}))
    turn = send(wo_h, wo.at[c, g], t_s, t_r, turned)
    stay = pltpu.make_async_copy(wo_h, wo.at[c, g], t_s)

    @pl.when(apart)
    def _():
        turn.start()

    @pl.when(jnp.logical_not(apart))
    def _():
        stay.start()

    for one in gathers:
        one.wait_recv()
    total = prs[0]
    for i in range(1, 8):
        total = total + prs[i]
    me = y * 8 + e
    qall[me] = total.astype(BF16)
    order = (0, 2, 3, 1)

    def group(k):
        return y ^ order[k]

    for k in range(4):
        for o in range(1 if k == 0 else 0, 8):
            one = send(
                qall.at[me], qall.at[me], q_s.at[k * 8 + o], q_r.at[me], {"seq": at_y((e + o) % 8, group(k))}
            )
            one.start()
            sends.append(one)

    def spread_columns():
        pl.when(apart)(turn.wait_recv)
        pl.when(jnp.logical_not(apart))(stay.wait)
        for o in range(1, 16):
            one = send(wo.at[c, p], wo.at[c, p], w_s.at[o], w_r.at[p], {"seq": 2 * ((p + o) % 16) + c})
            one.start()
            sends.append(one)

    lane = lax.broadcasted_iota(jnp.int32, (128, 128), 1)
    qws, sbufs = (qw0, qw1), (s0, s1)

    def take_queries(k):
        for o in range(1 if k == 0 else 0, 8):
            at = group(k) * 8 + (e + o) % 8
            send(qall.at[s], qall.at[at], q_s.at[0], q_r.at[at], {"seq": (s + 1) % 32}).wait_recv()
        q = qall[pl.ds(group(k) * 8, 8)].reshape(128, 128).astype(F32) * LOG2E
        high = q.astype(BF16).astype(F32)
        low = q - high
        qw = qws[k % 2]
        for h in range(2):
            keep = (lane < HEAD) if h == 0 else (lane >= HEAD)
            qw[h * 128 : (h + 1) * 128, 0:128] = jnp.where(keep, high, 0.0).astype(BF16)
            qw[h * 128 : (h + 1) * 128, 128:256] = jnp.where(keep, low, 0.0).astype(BF16)

    def scores(k, i, top):
        keys = kbuf[pl.ds(i * CHUNK, CHUNK), :]
        keys = jnp.concatenate([keys, keys], axis=1)
        score = lax.dot_general(keys, qws[k % 2][...], NT, preferred_element_type=F32)
        left = lens[pl.ds(group(k), 1), :] - s * POS - i * CHUNK
        ok = lax.broadcasted_iota(jnp.int32, (CHUNK, 128), 0) < left
        score = jnp.concatenate(
            [jnp.where(ok, score[:, :128], NEG), jnp.where(ok, score[:, 128:], NEG)], axis=1
        )
        sbufs[k % 2][pl.ds(i * CHUNK, CHUNK), :] = score
        return jnp.maximum(top, score.reshape(CHUNK // WIDE, WIDE, 256).max(axis=0))

    def weigh(k, i, peak, acc):
        weights = jnp.exp2(sbufs[k % 2][pl.ds(i * CHUNK, CHUNK), :] - peak).astype(BF16)
        values = vt[:, pl.ds(pl.multiple_of(i * CHUNK, CHUNK), CHUNK)]
        return acc + jnp.dot(values, weights, preferred_element_type=F32)

    def deliver(k, peak, acc):
        total = acc[128:129, :]
        scale = 1.0 / total
        both = jnp.concatenate(
            [acc[0:64, 0:128] * scale[:, 0:128], acc[64:128, 128:256] * scale[:, 128:256]], axis=0
        )
        msg[k, :, 0:ROWS, :] = both.T.astype(BF16).reshape(8, ROWS, 128)
        level = peak + jnp.log2(total)
        high = level.astype(BF16).astype(F32)
        mid = (level - high).astype(BF16).astype(F32)
        low = level - high - mid
        rows = [v[:, h * 128 : (h + 1) * 128] for v in (high, mid, low) for h in range(2)]
        rows = jnp.concatenate(rows + [jnp.zeros((10, 128), F32)], axis=0).astype(BF16)
        for o in range(8):
            msg[k, o, ROWS : 2 * ROWS, :] = rows
        if k == 0:
            cmb[s] = msg[0, e]
        for o in range(1 if k == 0 else 0, 8):
            to = (e + o) % 8
            one = send(msg.at[k, to], cmb.at[s], m_s.at[k * 8 + o], m_r.at[s], {"seq": at_y(to, group(k))})
            one.start()
            sends.append(one)

    loads[5].wait()
    peak = None
    for stage in range(5):
        if stage < 4:
            take_queries(stage)
        if stage == 1:
            spread_columns()

        def step(i, carry, stage=stage, peak=peak):
            top, acc = carry
            if stage < 4:
                top = scores(stage, i, top)
            if stage > 0:
                acc = weigh(stage - 1, i, peak, acc)
            return top, acc

        top, acc = lax.fori_loop(
            0, POS // CHUNK, step, (jnp.full((WIDE, 256), NEG, F32), jnp.zeros((VROWS, 256), F32))
        )
        if stage > 0:
            deliver(stage - 1, peak, acc)
        if stage < 4:
            peak = jnp.max(top, axis=0, keepdims=True)

    for o in range(1, 16):
        at = (p + o) % 16
        send(wo.at[c, at], wo.at[c, at], w_s.at[0], w_r.at[at], {"seq": (s + 1) % 32}).wait_recv()
    swap = send(wo.at[c], wo.at[c], c_s, c_r, {"seq": s + 1 - 2 * c})
    swap.start()
    sends.append(swap)

    for o in range(1, 32):
        at = (s + o) % 32
        send(cmb.at[at], cmb.at[at], m_s.at[0], m_r.at[at], {"seq": (s + 1) % 32}).wait_recv()
    level = jnp.dot(pick[...], cmb[:, ROWS : 2 * ROWS, :].reshape(512, 128), preferred_element_type=F32)
    shares = []
    for h in range(2):
        one = level[h * 32 : (h + 1) * 32]
        one = jnp.exp2(one - jnp.max(one, axis=0, keepdims=True))
        shares.append(one / jnp.sum(one, axis=0, keepdims=True))
    share = jnp.concatenate(shares, axis=0)
    high = share.astype(BF16)
    low = (share - high.astype(F32)).astype(BF16)
    own = (
        lax.broadcasted_iota(jnp.int32, (ROWS, 128), 1) == e * ROWS + lax.broadcasted_iota(jnp.int32, (ROWS, 128), 0)
    ).astype(F32).astype(BF16)
    turned_share = lax.dot_general(own, high, NT, preferred_element_type=F32) + lax.dot_general(
        own, low, NT, preferred_element_type=F32
    )
    high = turned_share.astype(BF16)
    low = (turned_share - high.astype(F32)).astype(BF16)
    spread = jnp.dot(high, rep[...], preferred_element_type=F32) + jnp.dot(low, rep[...], preferred_element_type=F32)
    joined = jnp.zeros((ROWS, 128), F32)
    for i in range(32):
        joined = joined + spread[:, i * 128 : (i + 1) * 128] * cmb[i, 0:ROWS, :].astype(F32)
    att[g] = joined.astype(BF16)
    for o in range(1, 16):
        one = send(att.at[g], att.at[g], a_s.at[o], a_r.at[g], {"grp": (g + o) % 16})
        one.start()
        sends.append(one)
    send(wo.at[1 - c], wo.at[1 - c], c_s, c_r, {"seq": s + 1 - 2 * c}).wait_recv()
    for o in range(1, 16):
        at = (g + o) % 16
        send(att.at[at], att.at[at], a_s.at[0], a_r.at[at], {"grp": (g + 1) % 16}).wait_recv()
    attended = jnp.concatenate([att[i] for i in range(16)], axis=1)
    for h in range(2):
        mixed = jnp.dot(attended, wo[h].reshape(2048, 128), preferred_element_type=F32)
        base = hid[:, pl.ds(pl.multiple_of(g * 256 + h * 128, 128), 128)].astype(F32)
        out[:, h * 128 : (h + 1) * 128] = (base + mixed).astype(BF16)

    for one in sends:
        one.wait_send()
    pl.when(apart)(turn.wait_send)


def body(hidden, norm_gain, w_query, w_out, enc_cache, lengths):
    dma = pltpu.SemaphoreType.DMA
    vm = pltpu.VMEM
    any_space = pl.BlockSpec(memory_space=pl.ANY)
    return pl.pallas_call(
        kernel,
        out_shape=jax.ShapeDtypeStruct((ROWS, 256), BF16),
        in_specs=[any_space] * 6,
        out_specs=pl.BlockSpec(memory_space=pltpu.VMEM),
        scratch_shapes=[
            vm((ROWS, 4096), BF16), vm((1, 4096), F32), vm((128, 128), BF16), vm((4, 128), jnp.int32), vm((4, 128), jnp.int32),
            vm((POS, 128), BF16), vm((POS, 128), BF16), vm((VROWS, POS), BF16),
            vm((8, ROWS, 512), BF16), vm((8, ROWS, 512), BF16), vm((4, 128, 128), BF16),
            vm((8, ROWS, 128), F32), vm((8, ROWS, 128), F32), vm((32, ROWS, 128), BF16),
            vm((256, 256), BF16), vm((256, 256), BF16), vm((POS, 256), F32), vm((POS, 256), F32),
            vm((4, 8, 2 * ROWS, 128), BF16), vm((32, 2 * ROWS, 128), BF16), vm((64, 4096), BF16), vm((64, 512), BF16),
            vm((16, ROWS, 128), BF16), vm((2, 16, 128, 128), BF16),
            dma((6,)), dma((4,)), dma((4,)), dma((8,)), dma((8,)), dma((8,)), dma((8,)), dma((32,)), dma((32,)),
            dma((32,)), dma((32,)), dma((16,)), dma((16,)), dma, dma, dma((16,)), dma((16,)), dma, dma,
        ],
        compiler_params=pltpu.CompilerParams(
            collective_id=0, has_side_effects=True, vmem_limit_bytes=56 * 2**20
        ),
        cost_estimate=pl.CostEstimate(flops=2200000000, bytes_accessed=6000000, transcendentals=8400000),
    )(hidden, norm_gain.reshape(1, 4096), w_query, w_out, enc_cache, lengths.reshape(4, 128))


def solution(mesh):
    placed = (P("seq", None), P(), P("seq", "grp"), P("grp", "seq"), P(None, "seq", "grp"), P())
    return jax.shard_map(body, mesh=mesh, in_specs=placed, out_specs=P("seq", "grp"), check_vma=False)
```

```python
import jax
import jax.numpy as jnp
from jax import lax
from jax.experimental import pallas as pl
from jax.experimental.pallas import tpu as pltpu
from jax.sharding import PartitionSpec as P

MESH = pl.DeviceIdType.MESH
F32 = jnp.float32
BF16 = jnp.bfloat16
NT = (((1,), (1,)), ((), ()))
LOG2E = 1.4426950408889634
NEG = -1e30
FOURTH = 2
HEAD = 64
ROWS = 16
POS = 8192
CHUNK = 4096
WIDE = 64
VROWS = 144


def kernel(
    hid_h, gain_h, wq_h, wo_h, enc_h, len_h, out,
    hid, gain, wq, lens_in, lens, kbuf, vbuf, vt, nrm, nra, wqa, prt, prs, qall, qw0, qw1, s0, s1,
    msg, cmb, rep, pick, att, wo,
    load, wq_s, wq_r, nr_s, nr_r, ps_s, ps_r, q_s, q_r, m_s, m_r, a_s, a_r, t_s, t_r, w_s, w_r, c_s, c_r,
):
    s, g = lax.axis_index("seq"), lax.axis_index("grp")
    x, y, p, c = s // 8, (s // 2) % 4, s // 2, s % 2
    e = x * 2 + c
    apart = p != g
    turned = {"seq": 2 * g + c, "grp": p}

    def at_y(place, row):
        return (place // 2) * 8 + row * 2 + place % 2

    def send(src, dst, ssem, rsem, where):
        return pltpu.make_async_remote_copy(
            src_ref=src, dst_ref=dst, send_sem=ssem, recv_sem=rsem, device_id=where, device_id_type=MESH
        )

    loads = [
        pltpu.make_async_copy(a, b, load.at[i])
        for i, (a, b) in enumerate(
            [(hid_h, hid), (gain_h, gain), (wq_h, wq), (len_h, lens_in), (enc_h.at[1], vbuf), (enc_h.at[0], kbuf)]
        )
    ]
    for one in loads:
        one.start()
    barrier = pltpu.get_barrier_semaphore()
    for o in range(1, 8):
        pl.semaphore_signal(barrier, inc=1, device_id={"seq": at_y((e + o) % 8, y)}, device_id_type=MESH)
    for o in range(1, 4):
        pl.semaphore_signal(barrier, inc=1, device_id={"seq": at_y(e, (y + o) % 4)}, device_id_type=MESH)
    for o in range(1, 16):
        pl.semaphore_signal(barrier, inc=1, device_id={"grp": (g + o) % 16}, device_id_type=MESH)

    @pl.when(apart)
    def _():
        pl.semaphore_signal(barrier, inc=1, device_id=turned, device_id_type=MESH)

    loads[0].wait()
    loads[1].wait()
    loads[2].wait()
    wide = hid[...].astype(F32)
    scale = lax.rsqrt(jnp.mean(wide * wide, axis=-1, keepdims=True) + 1e-06)
    normed = (wide * scale * gain[...]).astype(BF16)
    for i in range(8):
        nrm[i] = jnp.concatenate([normed[:, at_y(i, j) * 128 : at_y(i, j) * 128 + 128] for j in range(4)], axis=1)
    nra[e] = nrm[e]
    wqa[y] = wq[...]

    pl.semaphore_wait(barrier, 25 + apart.astype(jnp.int32))

    gathers, sends = [], []
    for o in range(1, 4):
        to, other = (y + o) % 4, (y + 4 - o) % 4
        sends.append(send(wq, wqa.at[y], wq_s.at[o], wq_r.at[y], {"seq": at_y(e, to)}))
        gathers.append(send(wq, wqa.at[other], wq_s.at[o], wq_r.at[other], {"seq": at_y(e, to)}))
    for o in range(1, 8):
        to, other = (e + o) % 8, (e + 8 - o) % 8
        sends.append(send(nrm.at[to], nra.at[e], nr_s.at[o], nr_r.at[e], {"seq": at_y(to, y)}))
        gathers.append(send(nrm.at[to], nra.at[other], nr_s.at[o], nr_r.at[other], {"seq": at_y(to, y)}))
    for one in sends:
        one.start()

    turn = send(wo_h, wo.at[c, g], t_s, t_r, turned)
    stay = pltpu.make_async_copy(wo_h, wo.at[c, g], t_s)

    @pl.when(apart)
    def _():
        turn.start()

    @pl.when(jnp.logical_not(apart))
    def _():
        stay.start()

    loads[4].wait()
    for i in range(8):
        vt[0:128, i * 1024 : (i + 1) * 1024] = vbuf[i * 1024 : (i + 1) * 1024, :].T
    vt[128:VROWS, :] = jnp.ones((VROWS - 128, POS), BF16)
    row = lax.broadcasted_iota(jnp.int32, (64, 4096), 0)
    col = lax.broadcasted_iota(jnp.int32, (64, 4096), 1)
    rep[...] = ((row % 32 == col // 128) & (row // 32 == (col % 128) // HEAD)).astype(F32).astype(BF16)
    row = lax.broadcasted_iota(jnp.int32, (64, 512), 0)
    col = lax.broadcasted_iota(jnp.int32, (64, 512), 1)
    pick[...] = ((row % 32 == col // 16) & (col % 16 < 6) & (col % 2 == row // 32)).astype(F32).astype(BF16)
    loads[3].wait()
    for i in range(4):
        lens[i : i + 1, :] = jnp.concatenate([lens_in[j : j + 1, i * 32 : i * 32 + 32] for j in range(4)], axis=1)

    def spread_columns(part):
        if part == 0:
            pl.when(apart)(turn.wait_recv)
            pl.when(jnp.logical_not(apart))(stay.wait)
            for o in (2, 1, 3):
                one = send(wo.at[c, p], wo.at[c, p], w_s.at[o], w_r.at[y], {"seq": at_y(e, (y + o) % 4)})
                one.start()
                sends.append(one)
        if part == FOURTH:
            for o in range(1, 4):
                at = (y + o) % 4
                slot = wo.at[c, x * 4 + at]
                send(slot, slot, w_s.at[0], w_r.at[at], {"seq": (s + 1) % 32}).wait_recv()
            four = wo.at[c, pl.ds(x * 4, 4)]
            for o in (2, 1, 3):
                one = send(four, four, w_s.at[4 + o], w_r.at[4 + x], {"seq": ((x + o) % 4) * 8 + y * 2 + c})
                one.start()
                sends.append(one)

    for one in gathers:
        one.wait_recv()
    part = jnp.dot(nra[...].reshape(128, 512), wqa[...].reshape(512, 128), preferred_element_type=F32)
    prt[...] = part.reshape(8, ROWS, 128)
    prs[e] = prt[e]
    gathers = []
    for o in range(1, 8):
        to, other = (e + o) % 8, (e + 8 - o) % 8
        one = send(prt.at[to], prs.at[e], ps_s.at[o], ps_r.at[e], {"seq": at_y(to, y)})
        one.start()
        sends.append(one)
        gathers.append(send(prt.at[to], prs.at[other], ps_s.at[o], ps_r.at[other], {"seq": at_y(to, y)}))
    for one in gathers:
        one.wait_recv()
    total = prs[0]
    for i in range(1, 8):
        total = total + prs[i]
    me = y * 8 + e
    qall[me] = total.astype(BF16)
    order = (0, 2, 3, 1)

    far_first = (4, 5, 3, 6, 2, 7, 1, 0)

    def group(k):
        return y ^ order[k]

    for k in range(4):
        for o in far_first[: 7 if k == 0 else 8]:
            one = send(
                qall.at[me], qall.at[me], q_s.at[k * 8 + o], q_r.at[me], {"seq": at_y((e + o) % 8, group(k))}
            )
            one.start()
            sends.append(one)

    lane = lax.broadcasted_iota(jnp.int32, (128, 128), 1)
    qws, sbufs = (qw0, qw1), (s0, s1)

    def take_queries(k):
        for o in range(1 if k == 0 else 0, 8):
            at = group(k) * 8 + (e + o) % 8
            send(qall.at[s], qall.at[at], q_s.at[0], q_r.at[at], {"seq": (s + 1) % 32}).wait_recv()
        q = qall[pl.ds(group(k) * 8, 8)].reshape(128, 128).astype(F32) * LOG2E
        high = q.astype(BF16).astype(F32)
        low = q - high
        qw = qws[k % 2]
        for h in range(2):
            keep = (lane < HEAD) if h == 0 else (lane >= HEAD)
            qw[h * 128 : (h + 1) * 128, 0:128] = jnp.where(keep, high, 0.0).astype(BF16)
            qw[h * 128 : (h + 1) * 128, 128:256] = jnp.where(keep, low, 0.0).astype(BF16)

    def scores(k, i, top):
        keys = kbuf[pl.ds(i * CHUNK, CHUNK), :]
        keys = jnp.concatenate([keys, keys], axis=1)
        score = lax.dot_general(keys, qws[k % 2][...], NT, preferred_element_type=F32)
        left = lens[pl.ds(group(k), 1), :] - s * POS - i * CHUNK
        ok = lax.broadcasted_iota(jnp.int32, (CHUNK, 128), 0) < left
        score = jnp.concatenate(
            [jnp.where(ok, score[:, :128], NEG), jnp.where(ok, score[:, 128:], NEG)], axis=1
        )
        sbufs[k % 2][pl.ds(i * CHUNK, CHUNK), :] = score
        return jnp.maximum(top, score.reshape(CHUNK // WIDE, WIDE, 256).max(axis=0))

    def weigh(k, i, peak, acc):
        weights = jnp.exp2(sbufs[k % 2][pl.ds(i * CHUNK, CHUNK), :] - peak).astype(BF16)
        values = vt[:, pl.ds(pl.multiple_of(i * CHUNK, CHUNK), CHUNK)]
        return acc + jnp.dot(values, weights, preferred_element_type=F32)

    def deliver(k, peak, acc):
        total = acc[128:129, :]
        scale = 1.0 / total
        both = jnp.concatenate(
            [acc[0:64, 0:128] * scale[:, 0:128], acc[64:128, 128:256] * scale[:, 128:256]], axis=0
        )
        msg[k, :, 0:ROWS, :] = both.T.astype(BF16).reshape(8, ROWS, 128)
        level = peak + jnp.log2(total)
        high = level.astype(BF16).astype(F32)
        mid = (level - high).astype(BF16).astype(F32)
        low = level - high - mid
        rows = [v[:, h * 128 : (h + 1) * 128] for v in (high, mid, low) for h in range(2)]
        rows = jnp.concatenate(rows + [jnp.zeros((10, 128), F32)], axis=0).astype(BF16)
        for o in range(8):
            msg[k, o, ROWS : 2 * ROWS, :] = rows
        if k == 0:
            cmb[s] = msg[0, e]
        for o in far_first[: 7 if k == 0 else 8]:
            to = (e + o) % 8
            one = send(msg.at[k, to], cmb.at[s], m_s.at[k * 8 + o], m_r.at[s], {"seq": at_y(to, group(k))})
            one.start()
            sends.append(one)

    loads[5].wait()
    peak = None
    for stage in range(5):
        if stage < 4:
            take_queries(stage)
            if stage < 3:
                spread_columns(stage)

        def step(i, carry, stage=stage, peak=peak):
            top, acc = carry
            if stage < 4:
                top = scores(stage, i, top)
            if stage > 0:
                acc = weigh(stage - 1, i, peak, acc)
            return top, acc

        top, acc = lax.fori_loop(
            0, POS // CHUNK, step, (jnp.full((WIDE, 256), NEG, F32), jnp.zeros((VROWS, 256), F32))
        )
        if stage > 0:
            deliver(stage - 1, peak, acc)
        if stage < 4:
            peak = jnp.max(top, axis=0, keepdims=True)

    for o in range(1, 4):
        at = (x + o) % 4
        four = wo.at[c, pl.ds(at * 4, 4)]
        send(four, four, w_s.at[0], w_r.at[4 + at], {"seq": (s + 1) % 32}).wait_recv()
    swap = send(wo.at[c], wo.at[c], c_s, c_r, {"seq": s + 1 - 2 * c})
    swap.start()
    sends.append(swap)

    for o in range(1, 32):
        at = (s + o) % 32
        send(cmb.at[at], cmb.at[at], m_s.at[0], m_r.at[at], {"seq": (s + 1) % 32}).wait_recv()
    level = jnp.dot(pick[...], cmb[:, ROWS : 2 * ROWS, :].reshape(512, 128), preferred_element_type=F32)
    shares = []
    for h in range(2):
        one = level[h * 32 : (h + 1) * 32]
        one = jnp.exp2(one - jnp.max(one, axis=0, keepdims=True))
        shares.append(one / jnp.sum(one, axis=0, keepdims=True))
    share = jnp.concatenate(shares, axis=0)
    high = share.astype(BF16)
    low = (share - high.astype(F32)).astype(BF16)
    own = (
        lax.broadcasted_iota(jnp.int32, (ROWS, 128), 1) == e * ROWS + lax.broadcasted_iota(jnp.int32, (ROWS, 128), 0)
    ).astype(F32).astype(BF16)
    turned_share = lax.dot_general(own, high, NT, preferred_element_type=F32) + lax.dot_general(
        own, low, NT, preferred_element_type=F32
    )
    high = turned_share.astype(BF16)
    low = (turned_share - high.astype(F32)).astype(BF16)
    spread = jnp.dot(high, rep[...], preferred_element_type=F32) + jnp.dot(low, rep[...], preferred_element_type=F32)
    joined = jnp.zeros((ROWS, 128), F32)
    for i in range(32):
        joined = joined + spread[:, i * 128 : (i + 1) * 128] * cmb[i, 0:ROWS, :].astype(F32)
    att[g] = joined.astype(BF16)
    for o in (9, 7, 8, 11, 5, 10, 6, 13, 3, 12, 4, 15, 1, 14, 2):
        one = send(att.at[g], att.at[g], a_s.at[o], a_r.at[g], {"grp": (g + o) % 16})
        one.start()
        sends.append(one)
    send(wo.at[1 - c], wo.at[1 - c], c_s, c_r, {"seq": s + 1 - 2 * c}).wait_recv()
    for o in range(1, 16):
        at = (g + o) % 16
        send(att.at[at], att.at[at], a_s.at[0], a_r.at[at], {"grp": (g + 1) % 16}).wait_recv()
    attended = jnp.concatenate([att[i] for i in range(16)], axis=1)
    for h in range(2):
        mixed = jnp.dot(attended, wo[h].reshape(2048, 128), preferred_element_type=F32)
        base = hid[:, pl.ds(pl.multiple_of(g * 256 + h * 128, 128), 128)].astype(F32)
        out[:, h * 128 : (h + 1) * 128] = (base + mixed).astype(BF16)

    for one in sends:
        one.wait_send()
    pl.when(apart)(turn.wait_send)


def body(hidden, norm_gain, w_query, w_out, enc_cache, lengths):
    dma = pltpu.SemaphoreType.DMA
    vm = pltpu.VMEM
    any_space = pl.BlockSpec(memory_space=pl.ANY)
    return pl.pallas_call(
        kernel,
        out_shape=jax.ShapeDtypeStruct((ROWS, 256), BF16),
        in_specs=[any_space] * 6,
        out_specs=pl.BlockSpec(memory_space=pltpu.VMEM),
        scratch_shapes=[
            vm((ROWS, 4096), BF16), vm((1, 4096), F32), vm((128, 128), BF16), vm((4, 128), jnp.int32), vm((4, 128), jnp.int32),
            vm((POS, 128), BF16), vm((POS, 128), BF16), vm((VROWS, POS), BF16),
            vm((8, ROWS, 512), BF16), vm((8, ROWS, 512), BF16), vm((4, 128, 128), BF16),
            vm((8, ROWS, 128), F32), vm((8, ROWS, 128), F32), vm((32, ROWS, 128), BF16),
            vm((256, 256), BF16), vm((256, 256), BF16), vm((POS, 256), F32), vm((POS, 256), F32),
            vm((4, 8, 2 * ROWS, 128), BF16), vm((32, 2 * ROWS, 128), BF16), vm((64, 4096), BF16), vm((64, 512), BF16),
            vm((16, ROWS, 128), BF16), vm((2, 16, 128, 128), BF16),
            dma((6,)), dma((4,)), dma((4,)), dma((8,)), dma((8,)), dma((8,)), dma((8,)), dma((32,)), dma((32,)),
            dma((32,)), dma((32,)), dma((16,)), dma((16,)), dma, dma, dma((16,)), dma((16,)), dma, dma,
        ],
        compiler_params=pltpu.CompilerParams(
            collective_id=0, has_side_effects=True, vmem_limit_bytes=56 * 2**20
        ),
        cost_estimate=pl.CostEstimate(flops=2200000000, bytes_accessed=6000000, transcendentals=8400000),
    )(hidden, norm_gain.reshape(1, 4096), w_query, w_out, enc_cache, lengths.reshape(4, 128))


def solution(mesh):
    placed = (P("seq", None), P(), P("seq", "grp"), P("grp", "seq"), P(None, "seq", "grp"), P())
    return jax.shard_map(body, mesh=mesh, in_specs=placed, out_specs=P("seq", "grp"), check_vma=False)
```
